512 devices in a mesh: head: 2 (over y_hi), inner: 32 (over y_lo, z), outer: 8 (over x, core).
Axes of the slice: x: 4, y: 4 (y_hi: 2, y_lo: 2; y = y_hi * 2 + y_lo), z: 16, core: 2. Of those that a mesh axis runs over, the one named last changes fastest.
Arguments:
- queries: bfloat16 [32768, 4096], P(('head', 'inner', 'outer')), may hold values from -6 to 6
- keys: bfloat16 [32768, 512], P(('head', 'inner', 'outer')), may hold values from -6 to 6
- values: bfloat16 [32768, 512], P(('head', 'inner', 'outer')), may hold values from -6 to 6
- block_order: int32 [2, 32, 8], replicated, may hold values from 0 to 511, as said below
Outputs:
- attended: bfloat16 [32768, 4096], P(('head', 'inner', 'outer'))
The draws below stay inside these ranges and needn't reach their ends.
Inputs may be any that keep to these rules, and one draw needn't show every extreme that they name: A permutation of the blocks: for each i and o, block_order[0, i, o] = o * 2 * 32 + c and block_order[1, i, o] = o * 2 * 32 + 2 * 32 - 1 - c, where c runs over a permutation of 0 to 31 for each o.
All inputs are finite; a program needn't handle non-finite values.
Results may differ from the reference program's by a relative error of at most 0.008.
Values may be sent and summed in bfloat16 or wider, within the bound.
No kernel may reach another device: no remote copies, remote signals or barrier semaphores. Data moves between devices by JAX's collectives and lax.ppermute only.
A program may use at most 64 MiB of HBM per device.

```python
import math
import jax
import jax.numpy as jnp
from jax import lax

HD = 128
QH = 32
KVH = 4
TOK_DEV = 64
GROUP = 8
STRETCH = 4096
SEQ = 32768
N_INNER = 32
N_OUTER = 8


def draw_queries(key, part):
    key = jax.random.fold_in(key, 1)
    drawn = jax.random.truncated_normal(key, -6.0, 6.0, (SEQ, QH * HD), jnp.float32)
    return drawn.astype(jnp.bfloat16)


def draw_keys(key, part):
    key = jax.random.fold_in(key, 2)
    drawn = jax.random.truncated_normal(key, -6.0, 6.0, (SEQ, KVH * HD), jnp.float32)
    return drawn.astype(jnp.bfloat16)


def draw_block_order(key, part):
    key = jax.random.fold_in(key, 3)
    shuffled = jax.vmap(lambda sub_key: jax.random.permutation(sub_key, jnp.arange(N_INNER, dtype=jnp.int32)))(jax.random.split(key, N_OUTER))
    stretch_first = (jnp.arange(N_OUTER, dtype=jnp.int32) * 2 * N_INNER)[:, None]
    lower_half = stretch_first + shuffled
    upper_half = stretch_first + 2 * N_INNER - 1 - shuffled
    return jnp.stack([lower_half.T, upper_half.T]).astype(jnp.int32)


def level_of(own_key, extent, shards, smallest, largest):
    loudness = 1.0
    for dim, shards_of in shards:
        draws = jax.random.uniform(jax.random.fold_in(jax.random.fold_in(own_key, 6), dim), (shards_of,), jnp.float32, smallest / len(shards), largest / len(shards))
        loudness = loudness * jnp.repeat(jnp.exp(draws), extent[dim] // shards_of).reshape((-1,) + (1,) * (len(extent) - 1 - dim))
    return loudness


def normal_values(stream_key, dims, width, limit, shards=(), held_as=jnp.bfloat16):
    values = jax.random.normal(stream_key, dims, jnp.float32) * width
    if len(shards) > 0:
        values = level_of(stream_key, dims, shards, -0.22, 0.18) * values
    return jnp.clip(values, min=-limit, max=limit).astype(held_as)


def setup_inputs(seed: int = 0) -> dict:
    seeds = jax.random.split(jax.random.key(seed), 5)
    return {
        "queries": draw_queries(jax.random.fold_in(seeds[4], 71), 0),
        "keys": draw_keys(jax.random.fold_in(seeds[4], 71), 0),
        "values": normal_values(seeds[2], (SEQ, KVH * HD), 1.0, 6.0, ((0, 512),)),
        "block_order": draw_block_order(jax.random.fold_in(seeds[4], 71), 0),
    }


very_low = -1e+30

def attend_stretch(stretch_index, sorted_query, padded_key, padded_value):
    first_query = (stretch_index * STRETCH).astype(jnp.int32)
    half = STRETCH // 2
    span = STRETCH + half
    stretch_query = lax.dynamic_slice_in_dim(sorted_query, first_query, STRETCH, 0).reshape(STRETCH, KVH, GROUP, HD)
    stretch_key = lax.dynamic_slice_in_dim(padded_key, first_query, span, 0).reshape(span, KVH, HD)
    stretch_value = lax.dynamic_slice_in_dim(padded_value, first_query, span, 0).reshape(span, KVH, HD)
    query_position = first_query + jnp.arange(STRETCH, dtype=jnp.int32)
    key_position = first_query - half + jnp.arange(span, dtype=jnp.int32)
    visible = (key_position[None, :] <= query_position[:, None]) & (key_position[None, :] >= 0)

    def one_head(head_index):
        query_head = lax.dynamic_index_in_dim(stretch_query, head_index, 1, keepdims=False).astype(jnp.float32)
        key_head = lax.dynamic_index_in_dim(stretch_key, head_index, 1, keepdims=False).astype(jnp.float32)
        value_head = lax.dynamic_index_in_dim(stretch_value, head_index, 1, keepdims=False).astype(jnp.float32)
        scores = jnp.einsum('rgd,nd->grn', query_head, key_head, precision=lax.Precision.HIGHEST) * (1.0 / math.sqrt(HD))
        scores = jnp.where(visible[None], scores, very_low)
        row_max = lax.optimization_barrier(jnp.max(scores, axis=-1))
        expo = jnp.where(visible[None], jnp.exp(scores - row_max[..., None]), 0.0)
        totals = lax.optimization_barrier(jnp.sum(expo, axis=-1))
        weights = lax.optimization_barrier(expo.astype(jnp.bfloat16)).astype(jnp.float32)
        summed = jnp.einsum('grn,nd->grd', weights, value_head, precision=lax.Precision.HIGHEST)
        return summed / totals[..., None]
    heads_out = lax.map(one_head, jnp.arange(KVH, dtype=jnp.int32))
    return heads_out.transpose(2, 0, 1, 3).reshape(STRETCH, QH * HD)

def reference(queries, keys, values, block_order):
    seq_total = queries.shape[0]
    row_index = jnp.arange(seq_total, dtype=jnp.int32)
    position = block_order.reshape(-1)[row_index // TOK_DEV] * TOK_DEV + row_index % TOK_DEV
    storage = jnp.zeros((seq_total,), jnp.int32).at[position].set(row_index)
    sorted_query = queries[storage]
    padded_key = jnp.concatenate([jnp.zeros((STRETCH // 2, KVH * HD), jnp.bfloat16), keys[storage]], axis=0)
    padded_value = jnp.concatenate([jnp.zeros((STRETCH // 2, KVH * HD), jnp.bfloat16), values[storage]], axis=0)
    stretches_out = lax.map(lambda stretch_index: attend_stretch(stretch_index, sorted_query, padded_key, padded_value), jnp.arange(seq_total // STRETCH, dtype=jnp.int32))
    attended_sorted = stretches_out.reshape(seq_total, QH * HD).astype(jnp.bfloat16)
    return attended_sorted[position]
```

```python
import functools
import math

import jax
import jax.numpy as jnp
from jax import lax
from jax.experimental import pallas as pl
from jax.experimental.pallas import tpu as pltpu
from jax.sharding import Mesh
from jax.sharding import PartitionSpec as P

HD = 128
TOK = 64
KVH = 4
GROUP = 8
ROWS = GROUP * TOK
CHUNK = 256
PER_CHUNK = CHUNK // TOK
LOW = -1e30
SCALE = math.log2(math.e) / math.sqrt(HD)

AXES = ("yh", "yl", "zh", "zp", "x", "c")
LINE = ("yh", "yl")
SHARE = ("yh", "yl", "zp")
RING = "zh"
STRETCHES = ("x", "c")
MIB = 1024 * 1024


def stacked_heads(q_ref, b):
    return jnp.concatenate(
        [q_ref[b, :, h * HD : (h + 1) * HD] for h in range(GROUP)], axis=0
    )


def fold(query, keys, values_t, visible, top_ref, total_ref, sum_ref, b):
    scores = lax.dot_general(
        keys, query, (((1,), (1,)), ((), ())), preferred_element_type=jnp.float32
    )
    if visible is not None:
        scores = jnp.where(visible, scores, LOW)
    old = top_ref[b]
    new = jnp.maximum(old, jnp.max(scores, axis=0, keepdims=True))
    weights = jnp.exp2((scores - new) * SCALE)
    factor = jnp.exp2((old - new) * SCALE)
    top_ref[b] = new
    total_ref[b] = total_ref[b] * factor + jnp.sum(weights, axis=0, keepdims=True)
    sum_ref[b] = sum_ref[b] * factor + jnp.dot(
        values_t, weights.astype(jnp.bfloat16), preferred_element_type=jnp.float32
    )


def earlier_kernel(info_ref, q_ref, kv_ref, top_ref, total_ref, sum_ref, k_s, vt_s):
    top_ref[...] = jnp.full(top_ref.shape, LOW, jnp.float32)
    total_ref[...] = jnp.zeros(total_ref.shape, jnp.float32)
    sum_ref[...] = jnp.zeros(sum_ref.shape, jnp.float32)
    chunks = vt_s.shape[0]

    @pl.when(info_ref[80] > 0)
    def _():
        flat = kv_ref[...].reshape(chunks * CHUNK, 2 * HD)
        for j in range(chunks):
            k_s[j] = flat[j * CHUNK : (j + 1) * CHUNK, :HD]
            vt_s[j] = flat[j * CHUNK : (j + 1) * CHUNK, HD:].T

        @pl.loop(0, q_ref.shape[0])
        def _(b):
            query = stacked_heads(q_ref, b)
            for j in range(chunks):
                fold(query, k_s[j], vt_s[j], None, top_ref, total_ref, sum_ref, b)


def own_kernel(
    info_ref, q_ref, kv_ref, top_in, total_in, sum_in, out_ref,
    top_ref, total_ref, sum_ref, k_s, v_s, vt_s,
):
    blocks = kv_ref.shape[0] * kv_ref.shape[1]
    across = kv_ref.shape[1]
    for i in range(blocks):
        at = pl.ds(pl.multiple_of(info_ref[i] * TOK, TOK), TOK)
        k_s[at, :] = kv_ref[i // across, i % across, :, :HD]
        v_s[at, :] = kv_ref[i // across, i % across, :, HD:]
    for j in range(vt_s.shape[0]):
        vt_s[j] = v_s[j * CHUNK : (j + 1) * CHUNK, :].T
    key_row = lax.broadcasted_iota(jnp.int32, (TOK, ROWS), 0)
    query_row = lax.broadcasted_iota(jnp.int32, (TOK, ROWS), 1) % TOK
    lead = query_row - key_row
    lane = lax.broadcasted_iota(jnp.int32, (TOK, HD), 1)

    @pl.loop(0, q_ref.shape[0])
    def _(b):
        top_ref[0] = top_in[b]
        total_ref[0] = total_in[b]
        sum_ref[0] = sum_in[b]
        query = stacked_heads(q_ref, b)
        own = info_ref[64 + b]
        seen = info_ref[72 + b]
        whole = info_ref[81 + b] // PER_CHUNK

        def keys_of(j):
            return k_s[pl.ds(pl.multiple_of(j * CHUNK, CHUNK), CHUNK), :]

        @pl.loop(0, whole)
        def _(j):
            fold(query, keys_of(j), vt_s[j], None, top_ref, total_ref, sum_ref, 0)

        @pl.when(seen > whole * PER_CHUNK)
        def _():
            visible = jnp.concatenate(
                [
                    lead >= (info_ref[32 + whole * PER_CHUNK + i] - own) * TOK
                    for i in range(PER_CHUNK)
                ],
                axis=0,
            )
            fold(query, keys_of(whole), vt_s[whole], visible, top_ref, total_ref, sum_ref, 0)

        total = total_ref[0]
        some = total > 0.0
        part = sum_ref[0] * jnp.where(some, 1.0 / jnp.where(some, total, 1.0), 0.0)
        part = part.T
        for h in range(GROUP):
            out_ref[b, :, h * HD : (h + 1) * HD] = part[h * TOK : (h + 1) * TOK].astype(
                jnp.bfloat16
            )
        level = jnp.where(some, top_ref[0] * SCALE + jnp.log2(jnp.where(some, total, 1.0)), LOW)
        level = jnp.broadcast_to(level, (HD, ROWS)).T
        picked = level[:TOK]
        for h in range(1, GROUP):
            picked = jnp.where(lane % GROUP == h, level[h * TOK : (h + 1) * TOK], picked)
        high = picked.astype(jnp.bfloat16).astype(jnp.float32)
        middle = (picked - high).astype(jnp.bfloat16).astype(jnp.float32)
        rest = picked - high - middle
        pieces = jnp.where(
            lane < GROUP,
            high,
            jnp.where(lane < 2 * GROUP, middle, jnp.where(lane < 3 * GROUP, rest, 0.0)),
        )
        out_ref[b, :, GROUP * HD :] = pieces.astype(jnp.bfloat16)


def join_kernel(parts_ref, out_ref):
    for m in range(KVH):
        level = []
        for p in range(2):
            pieces = parts_ref[2 * m + p, :, GROUP * HD :].astype(jnp.float32)
            level.append(
                pieces
                + pltpu.roll(pieces, HD - GROUP, 1)
                + pltpu.roll(pieces, HD - 2 * GROUP, 1)
            )
        share = 1.0 / (1.0 + jnp.exp2(level[1] - level[0]))
        for h in range(GROUP):
            first = parts_ref[2 * m, :, h * HD : (h + 1) * HD].astype(jnp.float32)
            second = parts_ref[2 * m + 1, :, h * HD : (h + 1) * HD].astype(jnp.float32)
            mixed = second + (first - second) * share[:, h : h + 1]
            at = (m * GROUP + h) * HD
            out_ref[:, at : at + HD] = mixed.astype(jnp.bfloat16)


def in_vmem():
    return pl.BlockSpec(memory_space=pltpu.VMEM)


def in_smem():
    return pl.BlockSpec(memory_space=pltpu.SMEM)


def tables(block_order):
    zh, zp = lax.axis_index("zh"), lax.axis_index("zp")
    stretch = lax.axis_index(STRETCHES)
    ids = lax.dynamic_index_in_dim(block_order, stretch, 2, keepdims=False)
    ids = ids.reshape(2, 2, lax.axis_size("zh"), lax.axis_size("zp"))
    keys = lax.dynamic_index_in_dim(ids, zp, 3, keepdims=False)
    keys = keys.transpose(2, 0, 1).reshape(-1)
    queries = lax.dynamic_index_in_dim(ids, zh, 2, keepdims=False).reshape(-1)
    place = jnp.sum(keys[None, :] < keys[:, None], axis=1, dtype=jnp.int32)
    slots = jnp.arange(keys.shape[0], dtype=jnp.int32)
    in_order = jnp.sum(jnp.where(place[None, :] == slots[:, None], keys[None, :], 0), axis=1)
    seen = jnp.sum(keys[None, :] <= queries[:, None], axis=1, dtype=jnp.int32)
    before = jnp.sum(keys[None, :] < queries[:, None], axis=1, dtype=jnp.int32)
    return jnp.concatenate([place, in_order, queries, seen, stretch.reshape(1), before])


def body(queries, keys, values, block_order):
    tokens = queries.shape[0]
    lines = KVH
    kv = jnp.stack(
        [
            jnp.concatenate(
                [keys[:, m * HD : (m + 1) * HD], values[:, m * HD : (m + 1) * HD]], axis=1
            )
            for m in range(lines)
        ]
    )
    own = lax.all_to_all(kv, LINE, split_axis=0, concat_axis=0, tiled=True)
    count = lax.axis_size("x") * lax.axis_size("c")
    earlier = lax.ppermute(own[2:], STRETCHES, [(i, i + 1) for i in range(count - 1)])
    own_all = lax.all_gather(own, RING, axis=0)
    earlier_all = lax.all_gather(earlier, RING, axis=0)
    info = tables(block_order)

    width = GROUP * HD
    split = queries.reshape(tokens, lines, width).transpose(1, 0, 2)
    pairs = lax.axis_size("zp")
    split = jnp.broadcast_to(split[:, None], (lines, pairs, tokens, width))
    split = split.reshape(lines * pairs, tokens, width)
    query = lax.all_to_all(split, SHARE, split_axis=0, concat_axis=0, tiled=True)
    blocks = lines * pairs

    rings = lax.axis_size(RING)
    chunks = rings * 2 * TOK // CHUNK
    state = [
        jax.ShapeDtypeStruct((blocks, 1, ROWS), jnp.float32),
        jax.ShapeDtypeStruct((blocks, 1, ROWS), jnp.float32),
        jax.ShapeDtypeStruct((blocks, HD, ROWS), jnp.float32),
    ]
    with jax.named_scope("earlier_part"):
        top, total, summed = pl.pallas_call(
            earlier_kernel,
            out_shape=state,
            in_specs=[in_smem(), in_vmem(), in_vmem()],
            out_specs=[in_vmem()] * 3,
            scratch_shapes=[
                pltpu.VMEM((chunks, CHUNK, HD), jnp.bfloat16),
                pltpu.VMEM((chunks, HD, CHUNK), jnp.bfloat16),
            ],
            compiler_params=pltpu.CompilerParams(vmem_limit_bytes=32 * MIB),
            cost_estimate=pl.CostEstimate(
                flops=4 * blocks * ROWS * chunks * CHUNK * HD,
                bytes_accessed=4 * MIB,
                transcendentals=blocks * ROWS * chunks * CHUNK,
            ),
        )(info, query, earlier_all)
    with jax.named_scope("own_part"):
        part = pl.pallas_call(
            own_kernel,
            out_shape=jax.ShapeDtypeStruct((blocks, tokens, width + HD), jnp.bfloat16),
            in_specs=[in_smem()] + [in_vmem()] * 5,
            out_specs=in_vmem(),
            scratch_shapes=[
                pltpu.VMEM((1, 1, ROWS), jnp.float32),
                pltpu.VMEM((1, 1, ROWS), jnp.float32),
                pltpu.VMEM((1, HD, ROWS), jnp.float32),
                pltpu.VMEM((2 * chunks * CHUNK, HD), jnp.bfloat16),
                pltpu.VMEM((2 * chunks * CHUNK, HD), jnp.bfloat16),
                pltpu.VMEM((2 * chunks, HD, CHUNK), jnp.bfloat16),
            ],
            compiler_params=pltpu.CompilerParams(vmem_limit_bytes=32 * MIB),
            cost_estimate=pl.CostEstimate(
                flops=4 * blocks * ROWS * chunks * CHUNK * HD,
                bytes_accessed=6 * MIB,
                transcendentals=blocks * ROWS * chunks * CHUNK,
            ),
        )(info, query, own_all, top, total, summed)
    parts = lax.all_to_all(part, SHARE, split_axis=0, concat_axis=0, tiled=True)
    with jax.named_scope("join_parts"):
        return pl.pallas_call(
            join_kernel,
            out_shape=jax.ShapeDtypeStruct((tokens, lines * width), jnp.bfloat16),
            in_specs=[in_vmem()],
            out_specs=in_vmem(),
            compiler_params=pltpu.CompilerParams(vmem_limit_bytes=32 * MIB),
            cost_estimate=pl.CostEstimate(
                flops=3 * tokens * lines * width, bytes_accessed=2 * MIB, transcendentals=0
            ),
        )(parts)


def solution(mesh):
    fine = Mesh(mesh.devices.reshape(2, 2, 8, 2, 4, 2), AXES)
    rows = P(AXES, None)
    return jax.shard_map(
        body, mesh=fine, in_specs=(rows, rows, rows, P()), out_specs=rows, check_vma=False
    )
```

```python
import functools
import math

import jax
import jax.numpy as jnp
from jax import lax
from jax.experimental import pallas as pl
from jax.experimental.pallas import tpu as pltpu
from jax.sharding import Mesh
from jax.sharding import PartitionSpec as P

HD = 128
TOK = 64
KVH = 4
GROUP = 8
ROWS = GROUP * TOK
CHUNK = 256
PER_CHUNK = CHUNK // TOK
LOW = -1e30
SCALE = math.log2(math.e) / math.sqrt(HD)

AXES = ("yh", "yl", "za", "zb", "zp", "x", "c")
LINE = ("yh", "yl")
SHARE = ("yh", "yl", "zp")
FAR = "za"
RING = ("za", "zb")
STRETCHES = ("x", "c")
ONWARD = ("za", "zb", "x", "c")
MIB = 1024 * 1024
ONES = 16
SIDE = HD + ONES


def stacked_heads(q_ref, b):
    return jnp.concatenate(
        [q_ref[b, :, h * HD : (h + 1) * HD] for h in range(GROUP)], axis=0
    )


def score(keys, query):
    return lax.dot_general(
        keys, query, (((1,), (1,)), ((), ())), preferred_element_type=jnp.float32
    )


def weigh(values_t, scores, top):
    weights = jnp.exp2((scores - top) * SCALE).astype(jnp.bfloat16)
    return jnp.dot(values_t, weights, preferred_element_type=jnp.float32)


def own_kernel(
    info_ref, q_ref, far_ref, next_ref, prev_ref, top_ref, total_ref, sum_ref,
    k_s, v_s, vt_s, lead_s, score_s, top_s, piece_s, piece_top,
):
    across = far_ref.shape[1]
    split = next_ref.shape[0]
    half = far_ref.shape[0] * across
    for i in range(2 * half):
        ring, line = (i % half) // across, i % across
        if i < half:
            block = far_ref[ring, line]
        elif ring < split:
            block = next_ref[ring, line]
        else:
            block = prev_ref[ring - split, line]
        at = pl.ds(pl.multiple_of(info_ref[i] * TOK, TOK), TOK)
        k_s[at, :] = block[:, :HD]
        v_s[at, :] = block[:, HD:]
    count = k_s.shape[0]
    for j in range(0, count, CHUNK):
        vt_s[:HD, j : j + CHUNK] = v_s[j : j + CHUNK, :].T
    vt_s[HD:, :] = jnp.ones((ONES, count), jnp.bfloat16)
    key_row = lax.broadcasted_iota(jnp.int32, (TOK, ROWS), 0)
    query_row = lax.broadcasted_iota(jnp.int32, (TOK, ROWS), 1) % TOK
    lead_s[...] = query_row - key_row
    pairs = q_ref.shape[0] // 2
    lower = count // 2
    top_ref[:pairs] = jnp.full((pairs, 1, ROWS), LOW, jnp.float32)
    total_ref[:pairs] = jnp.zeros((pairs, 1, ROWS), jnp.float32)
    sum_ref[:pairs] = jnp.zeros((pairs, HD, ROWS), jnp.float32)

    def begin(b, slot):
        scores = score(k_s[:lower, :], stacked_heads(q_ref, b))
        score_s[slot] = scores
        top_s[slot] = jnp.max(scores, axis=0, keepdims=True)

    def end(b, slot):
        top = top_s[slot]
        both = weigh(vt_s[:, :lower], score_s[slot], top)
        top_ref[b] = top
        total_ref[b] = both[HD : HD + 1]
        sum_ref[b] = both[:HD]

    begin(pairs, 0)

    @pl.loop(0, pairs // 2)
    def _(i):
        b = pairs + 2 * i
        begin(b + 1, 1)
        end(b, 0)
        begin(jnp.minimum(b + 2, 2 * pairs - 1), 0)
        end(b + 1, 1)

    steps = lower // CHUNK + 1
    items = pairs * steps

    def place(item):
        pair, step = item // steps, item % steps
        low = (info_ref[72 + pair] + PER_CHUNK - 1) // PER_CHUNK
        high = (info_ref[72 + pairs + pair] - lower // TOK + PER_CHUNK - 1) // PER_CHUNK
        is_low = step < low
        b = jnp.where(is_low, pair, pairs + pair)
        chunk = jnp.where(is_low, step, jnp.minimum(steps - 1 + step - low, 2 * steps - 3))
        own = jnp.where(step < low + high, info_ref[64 + b], -4096)
        return b, chunk, own

    def begin_item(item, slot):
        b, chunk, own = place(item)
        at = pl.ds(pl.multiple_of(chunk * CHUNK, CHUNK), CHUNK)
        scores = score(k_s[at, :], stacked_heads(q_ref, b))
        top = None
        for i in range(PER_CHUNK):
            ahead = (info_ref[32 + chunk * PER_CHUNK + i] - own) * TOK
            part = scores[i * TOK : (i + 1) * TOK]
            part = jnp.where(lead_s[...] >= ahead, part, LOW)
            piece_s[slot, i * TOK : (i + 1) * TOK, :] = part
            high = jnp.max(part, axis=0, keepdims=True)
            top = high if top is None else jnp.maximum(top, high)
        piece_top[slot] = top

    def end_item(item, slot):
        b, chunk, own = place(item)
        at = pl.ds(pl.multiple_of(chunk * CHUNK, CHUNK), CHUNK)
        old = top_ref[b]
        top = jnp.maximum(old, piece_top[slot])
        both = weigh(vt_s[:, at], piece_s[slot], top)
        factor = jnp.exp2((old - top) * SCALE)
        top_ref[b] = top
        total_ref[b] = total_ref[b] * factor + both[HD : HD + 1]
        sum_ref[b] = sum_ref[b] * factor + both[:HD]

    begin_item(0, 0)

    @pl.loop(0, items // 2)
    def _(i):
        begin_item(2 * i + 1, 1)
        end_item(2 * i, 0)
        begin_item(jnp.minimum(2 * i + 2, items - 1), 0)
        end_item(2 * i + 1, 1)


def earlier_kernel(
    info_ref, q_ref, far_ref, next_ref, prev_ref, top_in, total_in, sum_in, out_ref,
    k_s, vt_s, score_s, top_s,
):
    lane = lax.broadcasted_iota(jnp.int32, (TOK, HD), 1)

    def finish(b, top, total, summed):
        some = total > 0.0
        safe = jnp.where(some, total, 1.0)
        part = (summed * (1.0 / safe)).T
        for h in range(GROUP):
            out_ref[b, :, h * HD : (h + 1) * HD] = part[h * TOK : (h + 1) * TOK].astype(
                jnp.bfloat16
            )
        level = jnp.where(some, top * SCALE + jnp.log2(safe), LOW)
        level = jnp.broadcast_to(level, (HD, ROWS)).T
        picked = level[:TOK]
        for h in range(1, GROUP):
            picked = jnp.where(lane % GROUP == h, level[h * TOK : (h + 1) * TOK], picked)
        high = picked.astype(jnp.bfloat16).astype(jnp.float32)
        middle = (picked - high).astype(jnp.bfloat16).astype(jnp.float32)
        rest = picked - high - middle
        pieces = jnp.where(
            lane < GROUP,
            high,
            jnp.where(lane < 2 * GROUP, middle, jnp.where(lane < 3 * GROUP, rest, 0.0)),
        )
        out_ref[b, :, GROUP * HD :] = pieces.astype(jnp.bfloat16)

    blocks = q_ref.shape[0]

    @pl.when(info_ref[80] == 0)
    def _():
        @pl.loop(0, blocks)
        def _(b):
            finish(b, top_in[b], total_in[b], sum_in[b])

    @pl.when(info_ref[80] > 0)
    def _():
        at = 0
        for ref in (far_ref, next_ref, prev_ref):
            rows = ref.shape[0] * ref.shape[1] * TOK
            flat = ref[...].reshape(rows, 2 * HD)
            k_s[at : at + rows, :] = flat[:, :HD]
            for j in range(0, rows, CHUNK):
                vt_s[:HD, at + j : at + j + CHUNK] = flat[j : j + CHUNK, HD:].T
            at += rows
        vt_s[HD:, :] = jnp.ones((ONES, at), jnp.bfloat16)

        def begin(b, slot):
            scores = score(k_s[...], stacked_heads(q_ref, b))
            score_s[slot] = scores
            top_s[slot] = jnp.max(scores, axis=0, keepdims=True)

        def end(b, slot):
            old = top_in[b]
            top = jnp.maximum(old, top_s[slot])
            both = weigh(vt_s[...], score_s[slot], top)
            factor = jnp.exp2((old - top) * SCALE)
            finish(
                b,
                top,
                total_in[b] * factor + both[HD : HD + 1],
                sum_in[b] * factor + both[:HD],
            )

        begin(0, 0)

        @pl.loop(0, blocks // 2)
        def _(i):
            begin(2 * i + 1, 1)
            end(2 * i, 0)
            begin(jnp.minimum(2 * i + 2, blocks - 1), 0)
            end(2 * i + 1, 1)


def join_kernel(parts_ref, out_ref):
    for m in range(KVH):
        level = []
        for p in range(2):
            pieces = parts_ref[2 * m + p, :, GROUP * HD :].astype(jnp.float32)
            level.append(
                pieces
                + pltpu.roll(pieces, HD - GROUP, 1)
                + pltpu.roll(pieces, HD - 2 * GROUP, 1)
            )
        share = 1.0 / (1.0 + jnp.exp2(level[1] - level[0]))
        for h in range(GROUP):
            first = parts_ref[2 * m, :, h * HD : (h + 1) * HD].astype(jnp.float32)
            second = parts_ref[2 * m + 1, :, h * HD : (h + 1) * HD].astype(jnp.float32)
            mixed = second + (first - second) * share[:, h : h + 1]
            at = (m * GROUP + h) * HD
            out_ref[:, at : at + HD] = mixed.astype(jnp.bfloat16)


def in_vmem():
    return pl.BlockSpec(memory_space=pltpu.VMEM)


def in_smem():
    return pl.BlockSpec(memory_space=pltpu.SMEM)


def tables(block_order):
    za, zb, zp = (lax.axis_index(name) for name in ("za", "zb", "zp"))
    stretch = lax.axis_index(STRETCHES)
    ids = lax.dynamic_index_in_dim(block_order, stretch, 2, keepdims=False)
    ids = ids.reshape(2, 2, lax.axis_size("za"), lax.axis_size("zb"), lax.axis_size("zp"))
    keys = lax.dynamic_index_in_dim(ids, zp, 4, keepdims=False)
    near = lax.dynamic_index_in_dim(keys, zb, 3, keepdims=False)
    other = lax.dynamic_index_in_dim(keys, 1 - zb, 3, keepdims=False)
    keys = jnp.stack([near, other]).transpose(0, 3, 1, 2).reshape(-1)
    queries = lax.dynamic_index_in_dim(ids, za, 2, keepdims=False)
    queries = lax.dynamic_index_in_dim(queries, zb, 2, keepdims=False).reshape(-1)
    place = jnp.sum(keys[None, :] < keys[:, None], axis=1, dtype=jnp.int32)
    slots = jnp.arange(keys.shape[0], dtype=jnp.int32)
    in_order = jnp.sum(jnp.where(place[None, :] == slots[:, None], keys[None, :], 0), axis=1)
    seen = jnp.sum(keys[None, :] <= queries[:, None], axis=1, dtype=jnp.int32)
    return jnp.concatenate([place, in_order, queries, seen, stretch.reshape(1)])


def onward(block, step, stretches):
    ring = lax.axis_size(RING)
    outer = lax.axis_size(STRETCHES)
    route = [
        (r * outer + o, (r + step) % ring * outer + o + stretches)
        for r in range(ring)
        for o in range(outer - stretches)
    ]
    return lax.ppermute(block, ONWARD, route)


def body(queries, keys, values, block_order):
    tokens = queries.shape[0]
    lines = KVH
    kv = jnp.stack(
        [
            jnp.concatenate(
                [keys[:, m * HD : (m + 1) * HD], values[:, m * HD : (m + 1) * HD]], axis=1
            )
            for m in range(lines)
        ]
    )
    own = lax.all_to_all(kv, LINE, split_axis=0, concat_axis=0, tiled=True)
    far = lax.all_gather(own, FAR, axis=0)
    cut = far.shape[0] // 2
    upper = far[:, 2:]
    own_next = onward(far[:cut], -1, 0)
    own_prev = onward(far[cut:], 1, 0)
    earlier_far = onward(upper, 0, 1)
    earlier_next = onward(upper[:cut], -1, 1)
    earlier_prev = onward(upper[cut:], 1, 1)
    info = tables(block_order)

    width = GROUP * HD
    split = queries.reshape(tokens, lines, width).transpose(1, 0, 2)
    pairs = lax.axis_size("zp")
    split = jnp.broadcast_to(split[:, None], (lines, pairs, tokens, width))
    split = split.reshape(lines * pairs, tokens, width)
    query = lax.all_to_all(split, SHARE, split_axis=0, concat_axis=0, tiled=True)
    blocks = lines * pairs

    count = lax.axis_size(RING) * 2 * TOK
    state = [
        jax.ShapeDtypeStruct((blocks, 1, ROWS), jnp.float32),
        jax.ShapeDtypeStruct((blocks, 1, ROWS), jnp.float32),
        jax.ShapeDtypeStruct((blocks, HD, ROWS), jnp.float32),
    ]
    params = pltpu.CompilerParams(vmem_limit_bytes=40 * MIB)
    cost = pl.CostEstimate(
        flops=4 * blocks * ROWS * count * HD,
        bytes_accessed=4 * MIB,
        transcendentals=blocks * ROWS * count,
    )
    slots = [
        pltpu.VMEM((2, count, ROWS), jnp.float32),
        pltpu.VMEM((2, 1, ROWS), jnp.float32),
    ]
    with jax.named_scope("own_part"):
        top, total, summed = pl.pallas_call(
            own_kernel,
            out_shape=state,
            in_specs=[in_smem()] + [in_vmem()] * 4,
            out_specs=[in_vmem()] * 3,
            scratch_shapes=[
                pltpu.VMEM((2 * count, HD), jnp.bfloat16),
                pltpu.VMEM((2 * count, HD), jnp.bfloat16),
                pltpu.VMEM((SIDE, 2 * count), jnp.bfloat16),
                pltpu.VMEM((TOK, ROWS), jnp.int32),
                *slots,
                pltpu.VMEM((2, CHUNK, ROWS), jnp.float32),
                pltpu.VMEM((2, 1, ROWS), jnp.float32),
            ],
            compiler_params=params,
            cost_estimate=cost,
        )(info, query, far, own_next, own_prev)
    with jax.named_scope("earlier_part"):
        part = pl.pallas_call(
            earlier_kernel,
            out_shape=jax.ShapeDtypeStruct((blocks, tokens, width + HD), jnp.bfloat16),
            in_specs=[in_smem()] + [in_vmem()] * 7,
            out_specs=in_vmem(),
            scratch_shapes=[
                pltpu.VMEM((count, HD), jnp.bfloat16),
                pltpu.VMEM((SIDE, count), jnp.bfloat16),
                *slots,
            ],
            compiler_params=params,
            cost_estimate=cost,
        )(info, query, earlier_far, earlier_next, earlier_prev, top, total, summed)
    parts = lax.all_to_all(part, SHARE, split_axis=0, concat_axis=0, tiled=True)
    with jax.named_scope("join_parts"):
        return pl.pallas_call(
            join_kernel,
            out_shape=jax.ShapeDtypeStruct((tokens, lines * width), jnp.bfloat16),
            in_specs=[in_vmem()],
            out_specs=in_vmem(),
            compiler_params=params,
            cost_estimate=pl.CostEstimate(
                flops=3 * tokens * lines * width, bytes_accessed=2 * MIB, transcendentals=0
            ),
        )(parts)


def solution(mesh):
    fine = Mesh(mesh.devices.reshape(2, 2, 4, 2, 2, 4, 2), AXES)
    rows = P(AXES, None)
    return jax.shard_map(
        body, mesh=fine, in_specs=(rows, rows, rows, P()), out_specs=rows, check_vma=False
    )
```

```python
import functools
import math

import jax
import jax.numpy as jnp
from jax import lax
from jax.experimental import pallas as pl
from jax.experimental.pallas import tpu as pltpu
from jax.sharding import Mesh
from jax.sharding import PartitionSpec as P

HD = 128
TOK = 64
KVH = 4
GROUP = 8
ROWS = GROUP * TOK
CHUNK = 256
PER_CHUNK = CHUNK // TOK
LOW = -1e30
SCALE = math.log2(math.e) / math.sqrt(HD)

AXES = ("yh", "yl", "za", "zb", "zp", "x", "c")
LINE = ("yh", "yl")
SHARE = ("yh", "yl", "zp")
DEPTH = ("za", "zb", "zp")
RING = ("za", "zb")
STRETCHES = ("x", "c")
FAR = ((0, 4, 8, 12), (13, 9, 5, 1), (2, 6, 10, 14), (15, 11, 7, 3))
MIB = 1024 * 1024
ONES = 16
SIDE = HD + ONES
PARTS = 1
LEVELS = 16


def stacked_heads(q_ref, b, first=0, count=GROUP):
    return jnp.concatenate(
        [q_ref[b, :, h * HD : (h + 1) * HD] for h in range(first, first + count)], axis=0
    )


def score(keys, query):
    return lax.dot_general(
        keys, query, (((1,), (1,)), ((), ())), preferred_element_type=jnp.float32
    )


def weigh(values_t, scores, top):
    weights = jnp.exp2((scores - top) * SCALE).astype(jnp.bfloat16)
    return jnp.dot(values_t, weights, preferred_element_type=jnp.float32)


def pack_queries_kernel(q_ref, out_ref):
    width = GROUP * HD
    copies = out_ref.shape[0] // KVH
    for m in range(KVH):
        for i in range(copies):
            out_ref[m * copies + i] = q_ref[:, m * width : (m + 1) * width]


def own_kernel(first, info_ref, q_ref, lower_ref, upper_ref, *refs):
    if not first:
        state_in, refs = refs[:3], refs[3:]
    top_ref, total_ref, sum_ref, k_s, v_s, vt_s, lead_s, score_s, top_s, piece_s, piece_top = refs
    half = lower_ref.shape[0] * 2
    for i in range(2 * half):
        place, line = i % half // 2, i % 2
        block = (lower_ref if i < half else upper_ref)[place, line]
        at = pl.ds(pl.multiple_of(info_ref[i] * TOK, TOK), TOK)
        k_s[at, :] = block[:, :HD]
        v_s[at, :] = block[:, HD:]
    count = k_s.shape[0]
    for j in range(0, count, CHUNK):
        vt_s[:HD, j : j + CHUNK] = v_s[j : j + CHUNK, :].T
    vt_s[HD:, :] = jnp.ones((ONES, count), jnp.bfloat16)
    key_row = lax.broadcasted_iota(jnp.int32, (TOK, ROWS), 0)
    query_row = lax.broadcasted_iota(jnp.int32, (TOK, ROWS), 1) % TOK
    lead_s[...] = query_row - key_row
    blocks = q_ref.shape[0]
    pairs = blocks // 2
    lower = count // 2
    numbers, queries, seen = 2 * half, 4 * half, 4 * half + blocks
    if first:
        top_ref[...] = jnp.full(top_ref.shape, LOW, jnp.float32)
        total_ref[...] = jnp.zeros(total_ref.shape, jnp.float32)
        sum_ref[...] = jnp.zeros(sum_ref.shape, jnp.float32)
    else:
        for ref, ref_in in zip((top_ref, total_ref, sum_ref), state_in):
            ref[...] = ref_in[...]

    def add(b, values_t, scores, top_new):
        old = top_ref[b]
        top = jnp.maximum(old, top_new)
        both = weigh(values_t, scores, top)
        factor = jnp.exp2((old - top) * SCALE)
        top_ref[b] = top
        total_ref[b] = total_ref[b] * factor + both[HD : HD + 1]
        sum_ref[b] = sum_ref[b] * factor + both[:HD]

    def begin(b, slot):
        scores = score(k_s[:lower, :], stacked_heads(q_ref, b))
        score_s[slot] = scores
        top_s[slot] = jnp.max(scores, axis=0, keepdims=True)

    def end(b, slot):
        add(b, vt_s[:, :lower], score_s[slot], top_s[slot])

    steps = lower // CHUNK + 1
    items = pairs * steps

    def place_of(item):
        pair, step = item // steps, item % steps
        low = (info_ref[seen + pair] + PER_CHUNK - 1) // PER_CHUNK
        high = (info_ref[seen + pairs + pair] - half + PER_CHUNK - 1) // PER_CHUNK
        is_low = step < low
        b = jnp.where(is_low, pair, pairs + pair)
        chunk = jnp.where(is_low, step, jnp.minimum(steps - 1 + step - low, 2 * steps - 3))
        own = jnp.where(step < low + high, info_ref[queries + b], -4096)
        return b, chunk, own

    def begin_item(item, slot):
        b, chunk, own = place_of(item)
        at = pl.ds(pl.multiple_of(chunk * CHUNK, CHUNK), CHUNK)
        scores = score(k_s[at, :], stacked_heads(q_ref, b))
        top = None
        for i in range(PER_CHUNK):
            ahead = (info_ref[numbers + chunk * PER_CHUNK + i] - own) * TOK
            part = scores[i * TOK : (i + 1) * TOK]
            part = jnp.where(lead_s[...] >= ahead, part, LOW)
            piece_s[slot, i * TOK : (i + 1) * TOK, :] = part
            high = jnp.max(part, axis=0, keepdims=True)
            top = high if top is None else jnp.maximum(top, high)
        piece_top[slot] = top

    def end_item(item, slot):
        b, chunk, own = place_of(item)
        at = pl.ds(pl.multiple_of(chunk * CHUNK, CHUNK), CHUNK)
        add(b, vt_s[:, at], piece_s[slot], piece_top[slot])

    begin(pairs, 0)
    begin(pairs + 1, 1)
    begin(pairs + 2, 2)
    end(pairs, 0)
    begin(pairs + 3, 3)
    end(pairs + 1, 1)
    begin_item(0, 0)
    end(pairs + 2, 2)
    begin_item(1, 1)
    end(pairs + 3, 3)

    @pl.loop(0, items // 4)
    def _(i):
        begin_item(4 * i + 2, 2)
        begin_item(4 * i + 3, 3)
        end_item(4 * i, 0)
        end_item(4 * i + 1, 1)
        begin_item(jnp.minimum(4 * i + 4, items - 1), 0)
        begin_item(jnp.minimum(4 * i + 5, items - 1), 1)
        end_item(4 * i + 2, 2)
        end_item(4 * i + 3, 3)


def earlier_kernel(
    part, info_ref, q_ref, far_ref, prev_ref, top_in, total_in, sum_in, out_ref,
    k_s, vt_s, score_s, top_s,
):
    cols = score_s.shape[2]
    heads = cols // TOK
    here = slice(part * cols, (part + 1) * cols)

    def finish(b, top, total, summed):
        some = total > 0.0
        safe = jnp.where(some, total, 1.0)
        out_ref[b, :cols, :] = (summed * (1.0 / safe)).T.astype(jnp.bfloat16)
        level = jnp.where(some, top * SCALE + jnp.log2(safe), LOW)
        level = jnp.concatenate([level[:, j : j + HD] for j in range(0, cols, HD)], axis=0)
        high = level.astype(jnp.bfloat16).astype(jnp.float32)
        middle = (level - high).astype(jnp.bfloat16).astype(jnp.float32)
        unused = jnp.zeros((LEVELS - 3 * (cols // HD), HD), jnp.float32)
        pieces = jnp.concatenate([high, middle, level - high - middle, unused], axis=0)
        out_ref[b, cols:, :] = pieces.astype(jnp.bfloat16)

    blocks = q_ref.shape[0]

    @pl.when(info_ref[0] == 0)
    def _():
        @pl.loop(0, blocks)
        def _(b):
            finish(b, top_in[b, :, here], total_in[b, :, here], sum_in[b, :, here])

    @pl.when(info_ref[0] > 0)
    def _():
        at = 0
        for ref in (far_ref, prev_ref):
            rows = ref.shape[0] * ref.shape[1] * TOK
            flat = ref[...].reshape(rows, 2 * HD)
            k_s[at : at + rows, :] = flat[:, :HD]
            for j in range(0, rows, CHUNK):
                vt_s[:HD, at + j : at + j + CHUNK] = flat[j : j + CHUNK, HD:].T
            at += rows
        vt_s[HD:, :] = jnp.ones((ONES, at), jnp.bfloat16)

        def begin(b, slot):
            scores = score(k_s[...], stacked_heads(q_ref, b, part * heads, heads))
            score_s[slot] = scores
            top_s[slot] = jnp.max(scores, axis=0, keepdims=True)

        def end(b, slot):
            old = top_in[b, :, here]
            top = jnp.maximum(old, top_s[slot])
            both = weigh(vt_s[...], score_s[slot], top)
            factor = jnp.exp2((old - top) * SCALE)
            finish(
                b,
                top,
                total_in[b, :, here] * factor + both[HD : HD + 1],
                sum_in[b, :, here] * factor + both[:HD],
            )

        begin(0, 0)

        @pl.loop(0, blocks // 2)
        def _(i):
            begin(2 * i + 1, 1)
            end(2 * i, 0)
            begin(jnp.minimum(2 * i + 2, blocks - 1), 0)
            end(2 * i + 1, 1)


def join_kernel(*refs):
    parts_refs, out_ref = refs[:-1], refs[-1]
    cols = parts_refs[0].shape[1] - LEVELS
    rows, heads = cols // HD, cols // TOK
    for part, parts_ref in enumerate(parts_refs):
        for m in range(KVH):
            level = []
            for p in range(2):
                pieces = parts_ref[2 * m + p, cols:, :].astype(jnp.float32)
                level.append(
                    pieces[:rows] + pieces[rows : 2 * rows] + pieces[2 * rows : 3 * rows]
                )
            share = 1.0 / (1.0 + jnp.exp2(level[1] - level[0]))
            share = jnp.concatenate([share, jnp.zeros((8 - rows, HD), jnp.float32)], axis=0).T
            for h in range(heads):
                at = h * TOK
                first = parts_ref[2 * m, at : at + TOK, :].astype(jnp.float32)
                second = parts_ref[2 * m + 1, at : at + TOK, :].astype(jnp.float32)
                mine = share[at % HD : at % HD + TOK, at // HD : at // HD + 1]
                mixed = second + (first - second) * mine
                at = (m * GROUP + part * heads + h) * HD
                out_ref[:, at : at + HD] = mixed.astype(jnp.bfloat16)


def in_vmem():
    return pl.BlockSpec(memory_space=pltpu.VMEM)


def in_smem():
    return pl.BlockSpec(memory_space=pltpu.SMEM)


def tables(block_order):
    za, zb, zp = (lax.axis_index(name) for name in ("za", "zb", "zp"))
    stretch = lax.axis_index(STRETCHES)
    ids = lax.dynamic_index_in_dim(block_order, stretch, 2, keepdims=False)
    ids = ids.reshape(2, 2, lax.axis_size("za"), lax.axis_size("zb"), lax.axis_size("zp"))
    keys = lax.dynamic_index_in_dim(ids, zp, 4, keepdims=False)
    keys = jnp.where(zp == 1, keys[:, :, ::-1], keys)
    near = lax.dynamic_index_in_dim(keys, zb, 3, keepdims=False)
    other = lax.dynamic_index_in_dim(keys, 1 - zb, 3, keepdims=False)
    keys = jnp.stack([near, other]).transpose(0, 1, 3, 2).reshape(2, -1)
    queries = lax.dynamic_index_in_dim(ids, za, 2, keepdims=False)
    queries = lax.dynamic_index_in_dim(queries, zb, 2, keepdims=False).reshape(-1)
    place = jnp.sum(keys[:, None, :] < keys[:, :, None], axis=2, dtype=jnp.int32)
    slots = jnp.arange(keys.shape[1], dtype=jnp.int32)
    there = place[:, None, :] == slots[None, :, None]
    in_order = jnp.sum(jnp.where(there, keys[:, None, :], 0), axis=2)
    seen = jnp.sum(keys[:, None, :] <= queries[None, :, None], axis=2, dtype=jnp.int32)
    queries = jnp.broadcast_to(queries, seen.shape)
    table = jnp.concatenate([place, in_order, queries, seen], axis=1)
    return table[0], table[1], stretch.reshape(1)


def along(block, axis, step, around):
    count = lax.axis_size(axis)
    route = [(i, (i + step) % count) for i in range(count) if around or i + step < count]
    return lax.ppermute(block, axis, route)


def body(queries, keys, values, block_order):
    tokens = queries.shape[0]
    lines = KVH
    params = pltpu.CompilerParams(vmem_limit_bytes=40 * MIB)
    pairs = lax.axis_size("zp")
    width = GROUP * HD
    kv = jnp.stack(
        [
            jnp.concatenate(
                [keys[:, m * HD : (m + 1) * HD], values[:, m * HD : (m + 1) * HD]], axis=1
            )
            for m in range(lines)
        ]
    )
    own = lax.all_to_all(kv, LINE, split_axis=0, concat_axis=0, tiled=True)
    info_near, info_other, stretch = tables(block_order)

    with jax.named_scope("pack_queries"):
        split = pl.pallas_call(
            pack_queries_kernel,
            out_shape=jax.ShapeDtypeStruct((lines * pairs, tokens, width), jnp.bfloat16),
            in_specs=[in_vmem()],
            out_specs=in_vmem(),
            compiler_params=params,
            cost_estimate=pl.CostEstimate(flops=0, bytes_accessed=2 * MIB, transcendentals=0),
        )(queries)
    own, split, info_near, info_other, stretch = lax.optimization_barrier(
        (own, split, info_near, info_other, stretch)
    )
    far = lax.all_gather(own, DEPTH, axis=0, axis_index_groups=FAR)
    lower, upper = far[:, :2], far[:, 2:]
    own_next = along(lower, RING, -1, True)
    own_prev = along(upper, RING, 1, True)
    earlier_far = along(upper, STRETCHES, 1, False)
    earlier_prev = along(own_prev, STRETCHES, 1, False)
    query = lax.all_to_all(split, SHARE, split_axis=0, concat_axis=0, tiled=True)
    blocks = lines * pairs

    count = lax.axis_size(RING) * 2 * TOK
    state = [
        jax.ShapeDtypeStruct((blocks, 1, ROWS), jnp.float32),
        jax.ShapeDtypeStruct((blocks, 1, ROWS), jnp.float32),
        jax.ShapeDtypeStruct((blocks, HD, ROWS), jnp.float32),
    ]
    cost = pl.CostEstimate(
        flops=4 * blocks * ROWS * count * HD,
        bytes_accessed=4 * MIB,
        transcendentals=blocks * ROWS * count,
    )
    half = count // 2

    def own_part(first, info, lower, upper, *state_in):
        return pl.pallas_call(
            functools.partial(own_kernel, first),
            out_shape=state,
            in_specs=[in_smem()] + [in_vmem()] * (3 + len(state_in)),
            out_specs=[in_vmem()] * 3,
            scratch_shapes=[
                pltpu.VMEM((count, HD), jnp.bfloat16),
                pltpu.VMEM((count, HD), jnp.bfloat16),
                pltpu.VMEM((SIDE, count), jnp.bfloat16),
                pltpu.VMEM((TOK, ROWS), jnp.int32),
                pltpu.VMEM((4, half, ROWS), jnp.float32),
                pltpu.VMEM((4, 1, ROWS), jnp.float32),
                pltpu.VMEM((4, CHUNK, ROWS), jnp.float32),
                pltpu.VMEM((4, 1, ROWS), jnp.float32),
            ],
            compiler_params=params,
            cost_estimate=cost,
        )(info, query, lower, upper, *state_in)

    with jax.named_scope("own_near"):
        sums = own_part(True, info_near, lower, upper)
    with jax.named_scope("own_other"):
        sums = own_part(False, info_other, own_next, own_prev, *sums)
    cols = ROWS // PARTS
    joined = []
    for i in range(PARTS):
        with jax.named_scope("earlier_part"):
            part = pl.pallas_call(
                functools.partial(earlier_kernel, i),
                out_shape=jax.ShapeDtypeStruct((blocks, cols + LEVELS, HD), jnp.bfloat16),
                in_specs=[in_smem()] + [in_vmem()] * 6,
                out_specs=in_vmem(),
                scratch_shapes=[
                    pltpu.VMEM((count, HD), jnp.bfloat16),
                    pltpu.VMEM((SIDE, count), jnp.bfloat16),
                    pltpu.VMEM((2, count, cols), jnp.float32),
                    pltpu.VMEM((2, 1, cols), jnp.float32),
                ],
                compiler_params=params,
                cost_estimate=cost,
            )(stretch, query, earlier_far, earlier_prev, *sums)
        joined.append(lax.all_to_all(part, SHARE, split_axis=0, concat_axis=0, tiled=True))
    with jax.named_scope("join_parts"):
        return pl.pallas_call(
            join_kernel,
            out_shape=jax.ShapeDtypeStruct((tokens, lines * width), jnp.bfloat16),
            in_specs=[in_vmem()] * PARTS,
            out_specs=in_vmem(),
            compiler_params=params,
            cost_estimate=pl.CostEstimate(
                flops=3 * tokens * lines * width, bytes_accessed=2 * MIB, transcendentals=0
            ),
        )(*joined)


def solution(mesh):
    fine = Mesh(mesh.devices.reshape(2, 2, 4, 2, 2, 4, 2), AXES)
    rows = P(AXES, None)
    return jax.shard_map(
        body, mesh=fine, in_specs=(rows, rows, rows, P()), out_specs=rows, check_vma=False
    )
```

```python
import functools
import math

import jax
import jax.numpy as jnp
from jax import lax
from jax.experimental import pallas as pl
from jax.experimental.pallas import tpu as pltpu
from jax.sharding import Mesh
from jax.sharding import PartitionSpec as P

HD = 128
TOK = 64
KVH = 4
GROUP = 8
ROWS = GROUP * TOK
CHUNK = 256
PER_CHUNK = CHUNK // TOK
LOW = -1e30
SCALE = math.log2(math.e) / math.sqrt(HD)

AXES = ("yh", "yl", "za", "zb", "zp", "x", "c")
LINE = ("yh", "yl")
SHARE = ("yh", "yl", "zp")
DEPTH = ("za", "zb", "zp")
RING = ("za", "zb")
STRETCHES = ("x", "c")
FAR = ((0, 4, 8, 12), (13, 9, 5, 1), (2, 6, 10, 14), (15, 11, 7, 3))
MIB = 1024 * 1024
ONES = 16
SIDE = HD + ONES
PARTS = 1
LEVELS = 16


def stacked_heads(q_ref, b, first=0, count=GROUP):
    return jnp.concatenate(
        [q_ref[b, :, h * HD : (h + 1) * HD] for h in range(first, first + count)], axis=0
    )


def score(keys, query):
    return lax.dot_general(
        keys, query, (((1,), (1,)), ((), ())), preferred_element_type=jnp.float32
    )


def weigh(values_t, scores, top):
    weights = jnp.exp2((scores - top) * SCALE).astype(jnp.bfloat16)
    return jnp.dot(values_t, weights, preferred_element_type=jnp.float32)


def pack_queries_kernel(q_ref, out_ref):
    width = GROUP * HD
    copies = out_ref.shape[0] // KVH
    for m in range(KVH):
        for i in range(copies):
            out_ref[m * copies + i] = q_ref[:, m * width : (m + 1) * width]


def own_kernel(first, core, info_ref, *refs):
    if core is None:
        attend_own(first, info_ref, *refs)
    else:

        @pl.when(lax.rem(info_ref[info_ref.shape[0] - 1], 2) == core)
        def _():
            attend_own(first, info_ref, *refs)


def attend_own(first, info_ref, q_ref, lower_ref, upper_ref, *refs):
    if not first:
        state_0, state_1, refs = refs[:3], refs[3:6], refs[6:]
    top_ref, total_ref, sum_ref, k_s, v_s, vt_s, lead_s, score_s, top_s, piece_s, piece_top = refs
    half = lower_ref.shape[0] * 2
    for i in range(2 * half):
        place, line = i % half // 2, i % 2
        block = (lower_ref if i < half else upper_ref)[place, line]
        at = pl.ds(pl.multiple_of(info_ref[i] * TOK, TOK), TOK)
        k_s[at, :] = block[:, :HD]
        v_s[at, :] = block[:, HD:]
    count = k_s.shape[0]
    for j in range(0, count, CHUNK):
        vt_s[:HD, j : j + CHUNK] = v_s[j : j + CHUNK, :].T
    vt_s[HD:, :] = jnp.ones((ONES, count), jnp.bfloat16)
    key_row = lax.broadcasted_iota(jnp.int32, (TOK, ROWS), 0)
    query_row = lax.broadcasted_iota(jnp.int32, (TOK, ROWS), 1) % TOK
    lead_s[...] = query_row - key_row
    blocks = q_ref.shape[0]
    pairs = blocks // 2
    lower = count // 2
    numbers, queries, seen = 2 * half, 4 * half, 4 * half + blocks
    if first:
        top_ref[...] = jnp.full(top_ref.shape, LOW, jnp.float32)
        total_ref[...] = jnp.zeros(total_ref.shape, jnp.float32)
        sum_ref[...] = jnp.zeros(sum_ref.shape, jnp.float32)
    else:
        core = lax.rem(info_ref[info_ref.shape[0] - 1], 2)
        for at, state_in in enumerate((state_0, state_1)):

            @pl.when(core == at)
            def _(state_in=state_in):
                for ref, ref_in in zip((top_ref, total_ref, sum_ref), state_in):
                    ref[...] = ref_in[...]

    def add(b, values_t, scores, top_new):
        old = top_ref[b]
        top = jnp.maximum(old, top_new)
        both = weigh(values_t, scores, top)
        factor = jnp.exp2((old - top) * SCALE)
        top_ref[b] = top
        total_ref[b] = total_ref[b] * factor + both[HD : HD + 1]
        sum_ref[b] = sum_ref[b] * factor + both[:HD]

    def begin(b, slot):
        scores = score(k_s[:lower, :], stacked_heads(q_ref, b))
        score_s[slot] = scores
        top_s[slot] = jnp.max(scores, axis=0, keepdims=True)

    def end(b, slot):
        add(b, vt_s[:, :lower], score_s[slot], top_s[slot])

    steps = lower // CHUNK + 1
    items = pairs * steps

    def place_of(item):
        pair, step = item // steps, item % steps
        low = (info_ref[seen + pair] + PER_CHUNK - 1) // PER_CHUNK
        high = (info_ref[seen + pairs + pair] - half + PER_CHUNK - 1) // PER_CHUNK
        is_low = step < low
        b = jnp.where(is_low, pair, pairs + pair)
        chunk = jnp.where(is_low, step, jnp.minimum(steps - 1 + step - low, 2 * steps - 3))
        own = jnp.where(step < low + high, info_ref[queries + b], -4096)
        return b, chunk, own

    def begin_item(item, slot):
        b, chunk, own = place_of(item)
        at = pl.ds(pl.multiple_of(chunk * CHUNK, CHUNK), CHUNK)
        scores = score(k_s[at, :], stacked_heads(q_ref, b))
        top = None
        for i in range(PER_CHUNK):
            ahead = (info_ref[numbers + chunk * PER_CHUNK + i] - own) * TOK
            part = scores[i * TOK : (i + 1) * TOK]
            part = jnp.where(lead_s[...] >= ahead, part, LOW)
            piece_s[slot, i * TOK : (i + 1) * TOK, :] = part
            high = jnp.max(part, axis=0, keepdims=True)
            top = high if top is None else jnp.maximum(top, high)
        piece_top[slot] = top

    def end_item(item, slot):
        b, chunk, own = place_of(item)
        at = pl.ds(pl.multiple_of(chunk * CHUNK, CHUNK), CHUNK)
        add(b, vt_s[:, at], piece_s[slot], piece_top[slot])

    begin(pairs, 0)
    begin(pairs + 1, 1)
    begin(pairs + 2, 2)
    end(pairs, 0)
    begin(pairs + 3, 3)
    end(pairs + 1, 1)
    begin_item(0, 0)
    end(pairs + 2, 2)
    begin_item(1, 1)
    end(pairs + 3, 3)

    @pl.loop(0, items // 4)
    def _(i):
        begin_item(4 * i + 2, 2)
        begin_item(4 * i + 3, 3)
        end_item(4 * i, 0)
        end_item(4 * i + 1, 1)
        begin_item(jnp.minimum(4 * i + 4, items - 1), 0)
        begin_item(jnp.minimum(4 * i + 5, items - 1), 1)
        end_item(4 * i + 2, 2)
        end_item(4 * i + 3, 3)


def earlier_kernel(
    part, info_ref, q_ref, far_ref, prev_ref, top_in, total_in, sum_in, out_ref,
    k_s, vt_s, score_s, top_s,
):
    cols = score_s.shape[2]
    heads = cols // TOK
    here = slice(part * cols, (part + 1) * cols)

    def finish(b, top, total, summed):
        some = total > 0.0
        safe = jnp.where(some, total, 1.0)
        out_ref[b, :cols, :] = (summed * (1.0 / safe)).T.astype(jnp.bfloat16)
        level = jnp.where(some, top * SCALE + jnp.log2(safe), LOW)
        level = jnp.concatenate([level[:, j : j + HD] for j in range(0, cols, HD)], axis=0)
        high = level.astype(jnp.bfloat16).astype(jnp.float32)
        middle = (level - high).astype(jnp.bfloat16).astype(jnp.float32)
        unused = jnp.zeros((LEVELS - 3 * (cols // HD), HD), jnp.float32)
        pieces = jnp.concatenate([high, middle, level - high - middle, unused], axis=0)
        out_ref[b, cols:, :] = pieces.astype(jnp.bfloat16)

    blocks = q_ref.shape[0]

    @pl.when(info_ref[0] == 0)
    def _():
        @pl.loop(0, blocks)
        def _(b):
            finish(b, top_in[b, :, here], total_in[b, :, here], sum_in[b, :, here])

    @pl.when(info_ref[0] > 0)
    def _():
        at = 0
        for ref in (far_ref, prev_ref):
            rows = ref.shape[0] * ref.shape[1] * TOK
            flat = ref[...].reshape(rows, 2 * HD)
            k_s[at : at + rows, :] = flat[:, :HD]
            for j in range(0, rows, CHUNK):
                vt_s[:HD, at + j : at + j + CHUNK] = flat[j : j + CHUNK, HD:].T
            at += rows
        vt_s[HD:, :] = jnp.ones((ONES, at), jnp.bfloat16)

        def begin(b, slot):
            scores = score(k_s[...], stacked_heads(q_ref, b, part * heads, heads))
            score_s[slot] = scores
            top_s[slot] = jnp.max(scores, axis=0, keepdims=True)

        def end(b, slot):
            old = top_in[b, :, here]
            top = jnp.maximum(old, top_s[slot])
            both = weigh(vt_s[...], score_s[slot], top)
            factor = jnp.exp2((old - top) * SCALE)
            finish(
                b,
                top,
                total_in[b, :, here] * factor + both[HD : HD + 1],
                sum_in[b, :, here] * factor + both[:HD],
            )

        begin(0, 0)

        @pl.loop(0, blocks // 2)
        def _(i):
            begin(2 * i + 1, 1)
            end(2 * i, 0)
            begin(jnp.minimum(2 * i + 2, blocks - 1), 0)
            end(2 * i + 1, 1)


def join_kernel(*refs):
    parts_refs, out_ref = refs[:-1], refs[-1]
    cols = parts_refs[0].shape[1] - LEVELS
    rows, heads = cols // HD, cols // TOK
    for part, parts_ref in enumerate(parts_refs):
        for m in range(KVH):
            level = []
            for p in range(2):
                pieces = parts_ref[2 * m + p, cols:, :].astype(jnp.float32)
                level.append(
                    pieces[:rows] + pieces[rows : 2 * rows] + pieces[2 * rows : 3 * rows]
                )
            share = 1.0 / (1.0 + jnp.exp2(level[1] - level[0]))
            share = jnp.concatenate([share, jnp.zeros((8 - rows, HD), jnp.float32)], axis=0).T
            for h in range(heads):
                at = h * TOK
                first = parts_ref[2 * m, at : at + TOK, :].astype(jnp.float32)
                second = parts_ref[2 * m + 1, at : at + TOK, :].astype(jnp.float32)
                mine = share[at % HD : at % HD + TOK, at // HD : at // HD + 1]
                mixed = second + (first - second) * mine
                at = (m * GROUP + part * heads + h) * HD
                out_ref[:, at : at + HD] = mixed.astype(jnp.bfloat16)


def in_vmem():
    return pl.BlockSpec(memory_space=pltpu.VMEM)


def in_smem():
    return pl.BlockSpec(memory_space=pltpu.SMEM)


def tables(block_order):
    za, zb, zp = (lax.axis_index(name) for name in ("za", "zb", "zp"))
    stretch = lax.axis_index(STRETCHES)
    ids = lax.dynamic_index_in_dim(block_order, stretch, 2, keepdims=False)
    ids = ids.reshape(2, 2, lax.axis_size("za"), lax.axis_size("zb"), lax.axis_size("zp"))
    keys = lax.dynamic_index_in_dim(ids, zp, 4, keepdims=False)
    keys = jnp.where(zp == 1, keys[:, :, ::-1], keys)
    near = lax.dynamic_index_in_dim(keys, zb, 3, keepdims=False)
    other = lax.dynamic_index_in_dim(keys, 1 - zb, 3, keepdims=False)
    keys = jnp.stack([near, other]).transpose(0, 1, 3, 2).reshape(2, -1)
    queries = lax.dynamic_index_in_dim(ids, za, 2, keepdims=False)
    queries = lax.dynamic_index_in_dim(queries, zb, 2, keepdims=False).reshape(-1)
    place = jnp.sum(keys[:, None, :] < keys[:, :, None], axis=2, dtype=jnp.int32)
    slots = jnp.arange(keys.shape[1], dtype=jnp.int32)
    there = place[:, None, :] == slots[None, :, None]
    in_order = jnp.sum(jnp.where(there, keys[:, None, :], 0), axis=2)
    seen = jnp.sum(keys[:, None, :] <= queries[None, :, None], axis=2, dtype=jnp.int32)
    queries = jnp.broadcast_to(queries, seen.shape)
    stretches = jnp.broadcast_to(stretch, (2, 1))
    table = jnp.concatenate([place, in_order, queries, seen, stretches], axis=1)
    return table[0], table[1], stretch.reshape(1)


def along(block, axis, step, around):
    count = lax.axis_size(axis)
    route = [(i, (i + step) % count) for i in range(count) if around or i + step < count]
    return lax.ppermute(block, axis, route)


def body(queries, keys, values, block_order):
    tokens = queries.shape[0]
    lines = KVH
    params = pltpu.CompilerParams(vmem_limit_bytes=40 * MIB)
    pairs = lax.axis_size("zp")
    width = GROUP * HD
    kv = jnp.stack(
        [
            jnp.concatenate(
                [keys[:, m * HD : (m + 1) * HD], values[:, m * HD : (m + 1) * HD]], axis=1
            )
            for m in range(lines)
        ]
    )
    own = lax.all_to_all(kv, LINE, split_axis=0, concat_axis=0, tiled=True)
    info_near, info_other, stretch = tables(block_order)

    with jax.named_scope("pack_queries"):
        split = pl.pallas_call(
            pack_queries_kernel,
            out_shape=jax.ShapeDtypeStruct((lines * pairs, tokens, width), jnp.bfloat16),
            in_specs=[in_vmem()],
            out_specs=in_vmem(),
            compiler_params=params,
            cost_estimate=pl.CostEstimate(flops=0, bytes_accessed=2 * MIB, transcendentals=0),
        )(queries)
    own, split, info_near, info_other, stretch = lax.optimization_barrier(
        (own, split, info_near, info_other, stretch)
    )
    far = lax.all_gather(own, DEPTH, axis=0, axis_index_groups=FAR)
    lower, upper = far[:, :2], far[:, 2:]
    own_next = along(lower, RING, -1, True)
    own_prev = along(upper, RING, 1, True)
    query = lax.all_to_all(split, SHARE, split_axis=0, concat_axis=0, tiled=True)
    blocks = lines * pairs

    count = lax.axis_size(RING) * 2 * TOK
    state = [
        jax.ShapeDtypeStruct((blocks, 1, ROWS), jnp.float32),
        jax.ShapeDtypeStruct((blocks, 1, ROWS), jnp.float32),
        jax.ShapeDtypeStruct((blocks, HD, ROWS), jnp.float32),
    ]
    cost = pl.CostEstimate(
        flops=4 * blocks * ROWS * count * HD,
        bytes_accessed=4 * MIB,
        transcendentals=blocks * ROWS * count,
    )
    half = count // 2

    def own_part(core, info, lower, upper, *state_in):
        return pl.pallas_call(
            functools.partial(own_kernel, not state_in, core),
            out_shape=state,
            in_specs=[in_smem()] + [in_vmem()] * (3 + len(state_in)),
            out_specs=[in_vmem()] * 3,
            scratch_shapes=[
                pltpu.VMEM((count, HD), jnp.bfloat16),
                pltpu.VMEM((count, HD), jnp.bfloat16),
                pltpu.VMEM((SIDE, count), jnp.bfloat16),
                pltpu.VMEM((TOK, ROWS), jnp.int32),
                pltpu.VMEM((4, half, ROWS), jnp.float32),
                pltpu.VMEM((4, 1, ROWS), jnp.float32),
                pltpu.VMEM((4, CHUNK, ROWS), jnp.float32),
                pltpu.VMEM((4, 1, ROWS), jnp.float32),
            ],
            compiler_params=params,
            cost_estimate=cost,
        )(info, query, lower, upper, *state_in)

    with jax.named_scope("own_near_core_1"):
        sums_1 = own_part(1, info_near, lower, upper)
    onward, *sums_1 = lax.optimization_barrier((upper, *sums_1))
    own_prev, sums_1[0] = lax.optimization_barrier((own_prev, sums_1[0]))
    earlier_prev = along(own_prev, STRETCHES, 1, False)
    earlier_far = along(onward, STRETCHES, 1, False)
    own_prev, lower, upper = lax.optimization_barrier((own_prev, lower, upper))
    with jax.named_scope("own_near_core_0"):
        sums_0 = own_part(0, info_near, lower, upper)
    with jax.named_scope("own_other"):
        sums = own_part(None, info_other, own_next, own_prev, *sums_0, *sums_1)
    cols = ROWS // PARTS
    joined = []
    for i in range(PARTS):
        with jax.named_scope("earlier_part"):
            part = pl.pallas_call(
                functools.partial(earlier_kernel, i),
                out_shape=jax.ShapeDtypeStruct((blocks, cols + LEVELS, HD), jnp.bfloat16),
                in_specs=[in_smem()] + [in_vmem()] * 6,
                out_specs=in_vmem(),
                scratch_shapes=[
                    pltpu.VMEM((count, HD), jnp.bfloat16),
                    pltpu.VMEM((SIDE, count), jnp.bfloat16),
                    pltpu.VMEM((2, count, cols), jnp.float32),
                    pltpu.VMEM((2, 1, cols), jnp.float32),
                ],
                compiler_params=params,
                cost_estimate=cost,
            )(stretch, query, earlier_prev, earlier_far, *sums)
        joined.append(lax.all_to_all(part, SHARE, split_axis=0, concat_axis=0, tiled=True))
    with jax.named_scope("join_parts"):
        return pl.pallas_call(
            join_kernel,
            out_shape=jax.ShapeDtypeStruct((tokens, lines * width), jnp.bfloat16),
            in_specs=[in_vmem()] * PARTS,
            out_specs=in_vmem(),
            compiler_params=params,
            cost_estimate=pl.CostEstimate(
                flops=3 * tokens * lines * width, bytes_accessed=2 * MIB, transcendentals=0
            ),
        )(*joined)


def solution(mesh):
    fine = Mesh(mesh.devices.reshape(2, 2, 4, 2, 2, 4, 2), AXES)
    rows = P(AXES, None)
    return jax.shard_map(
        body, mesh=fine, in_specs=(rows, rows, rows, P()), out_specs=rows, check_vma=False
    )
```

```python
import functools
import math

import jax
import jax.numpy as jnp
from jax import lax
from jax.experimental import pallas as pl
from jax.experimental.pallas import tpu as pltpu
from jax.sharding import Mesh
from jax.sharding import PartitionSpec as P

HD = 128
TOK = 64
KVH = 4
GROUP = 8
ROWS = GROUP * TOK
CHUNK = 256
PER_CHUNK = CHUNK // TOK
LOW = -1e30
SCALE = math.log2(math.e) / math.sqrt(HD)

AXES = ("yh", "yl", "za", "zb", "zp", "x", "c")
LINE = ("yh", "yl")
SHARE = ("yh", "yl", "zp")
DEPTH = ("za", "zb", "zp")
RING = ("za", "zb")
STRETCHES = ("x", "c")
FAR = ((0, 4, 8, 12), (13, 9, 5, 1), (2, 6, 10, 14), (15, 11, 7, 3))
MIB = 1024 * 1024
ONES = 16
SIDE = HD + ONES
PARTS = 1
LEVELS = 16


def stacked_heads(q_ref, b, first=0, count=GROUP):
    return jnp.concatenate(
        [q_ref[b, :, h * HD : (h + 1) * HD] for h in range(first, first + count)], axis=0
    )


def score(keys, query):
    return lax.dot_general(
        keys, query, (((1,), (1,)), ((), ())), preferred_element_type=jnp.float32
    )


def weigh(values_t, scores, top):
    weights = jnp.exp2((scores - top) * SCALE).astype(jnp.bfloat16)
    return jnp.dot(values_t, weights, preferred_element_type=jnp.float32)


def pack_queries_kernel(q_ref, out_ref):
    width = GROUP * HD
    copies = out_ref.shape[0] // KVH
    for m in range(KVH):
        for i in range(copies):
            out_ref[m * copies + i] = q_ref[:, m * width : (m + 1) * width]


def core_of(info_ref):
    return lax.rem(info_ref[info_ref.shape[0] - 1], 2)


def own_kernel(stage, info_ref, *refs):
    if stage == 1:

        @pl.when(core_of(info_ref) == 0)
        def _():
            attend_own(stage, info_ref, *refs)

    else:
        attend_own(stage, info_ref, *refs)


def attend_own(stage, info_ref, q_ref, lower_ref, upper_ref, *refs):
    states = [refs[3 * i : 3 * i + 3] for i in range(stage)]
    refs = refs[3 * stage :]
    top_ref, total_ref, sum_ref, k_s, v_s, vt_s, lead_s, score_s, top_s, piece_s, piece_top = refs
    half = lower_ref.shape[0] * 2
    for i in range(2 * half):
        place, line = i % half // 2, i % 2
        block = (lower_ref if i < half else upper_ref)[place, line]
        at = pl.ds(pl.multiple_of(info_ref[i] * TOK, TOK), TOK)
        k_s[at, :] = block[:, :HD]
        v_s[at, :] = block[:, HD:]
    count = k_s.shape[0]
    for j in range(0, count, CHUNK):
        vt_s[:HD, j : j + CHUNK] = v_s[j : j + CHUNK, :].T
    vt_s[HD:, :] = jnp.ones((ONES, count), jnp.bfloat16)
    key_row = lax.broadcasted_iota(jnp.int32, (TOK, ROWS), 0)
    query_row = lax.broadcasted_iota(jnp.int32, (TOK, ROWS), 1) % TOK
    lead_s[...] = query_row - key_row
    blocks = q_ref.shape[0]
    pairs = blocks // 2
    lower = count // 2
    numbers, queries, seen = 2 * half, 4 * half, 4 * half + blocks
    if stage == 0:
        top_ref[...] = jnp.full(top_ref.shape, LOW, jnp.float32)
        total_ref[...] = jnp.zeros(total_ref.shape, jnp.float32)
        sum_ref[...] = jnp.zeros(sum_ref.shape, jnp.float32)
    for at, state in enumerate(states):

        @pl.when(core_of(info_ref) == at)
        def _(state=state):
            for ref, ref_in in zip((top_ref, total_ref, sum_ref), state):
                ref[...] = ref_in[...]

    def add(b, values_t, scores, top_new):
        old = top_ref[b]
        top = jnp.maximum(old, top_new)
        both = weigh(values_t, scores, top)
        factor = jnp.exp2((old - top) * SCALE)
        top_ref[b] = top
        total_ref[b] = total_ref[b] * factor + both[HD : HD + 1]
        sum_ref[b] = sum_ref[b] * factor + both[:HD]

    def begin(b, slot):
        scores = score(k_s[:lower, :], stacked_heads(q_ref, b))
        score_s[slot] = scores
        top_s[slot] = jnp.max(scores, axis=0, keepdims=True)

    def end(b, slot):
        add(b, vt_s[:, :lower], score_s[slot], top_s[slot])

    steps = lower // CHUNK + 1
    items = pairs * steps

    def place_of(item):
        pair, step = item // steps, item % steps
        low = (info_ref[seen + pair] + PER_CHUNK - 1) // PER_CHUNK
        high = (info_ref[seen + pairs + pair] - half + PER_CHUNK - 1) // PER_CHUNK
        is_low = step < low
        b = jnp.where(is_low, pair, pairs + pair)
        chunk = jnp.where(is_low, step, jnp.minimum(steps - 1 + step - low, 2 * steps - 3))
        own = jnp.where(step < low + high, info_ref[queries + b], -4096)
        return b, chunk, own

    def begin_item(item, slot):
        b, chunk, own = place_of(item)
        at = pl.ds(pl.multiple_of(chunk * CHUNK, CHUNK), CHUNK)
        scores = score(k_s[at, :], stacked_heads(q_ref, b))
        top = None
        for i in range(PER_CHUNK):
            ahead = (info_ref[numbers + chunk * PER_CHUNK + i] - own) * TOK
            part = scores[i * TOK : (i + 1) * TOK]
            part = jnp.where(lead_s[...] >= ahead, part, LOW)
            piece_s[slot, i * TOK : (i + 1) * TOK, :] = part
            high = jnp.max(part, axis=0, keepdims=True)
            top = high if top is None else jnp.maximum(top, high)
        piece_top[slot] = top

    def end_item(item, slot):
        b, chunk, own = place_of(item)
        at = pl.ds(pl.multiple_of(chunk * CHUNK, CHUNK), CHUNK)
        add(b, vt_s[:, at], piece_s[slot], piece_top[slot])

    if stage != 1:
        begin(pairs, 0)
        begin(pairs + 1, 1)
        begin(pairs + 2, 2)
        end(pairs, 0)
        begin(pairs + 3, 3)
        end(pairs + 1, 1)
    if stage == 2:
        begin_item(0, 0)
    if stage != 1:
        end(pairs + 2, 2)
    if stage == 2:
        begin_item(1, 1)
    if stage != 1:
        end(pairs + 3, 3)

    def all_items():
        if stage != 2:
            begin_item(0, 0)
            begin_item(1, 1)

        @pl.loop(0, items // 4)
        def _(i):
            begin_item(4 * i + 2, 2)
            begin_item(4 * i + 3, 3)
            end_item(4 * i, 0)
            end_item(4 * i + 1, 1)
            begin_item(jnp.minimum(4 * i + 4, items - 1), 0)
            begin_item(jnp.minimum(4 * i + 5, items - 1), 1)
            end_item(4 * i + 2, 2)
            end_item(4 * i + 3, 3)

    if stage == 0:
        pl.when(core_of(info_ref) == 1)(all_items)
    else:
        all_items()


def earlier_kernel(
    part, info_ref, q_ref, far_ref, prev_ref, top_in, total_in, sum_in, out_ref,
    k_s, vt_s, score_s, top_s,
):
    cols = score_s.shape[2]
    heads = cols // TOK
    here = slice(part * cols, (part + 1) * cols)

    def finish(b, top, total, summed):
        some = total > 0.0
        safe = jnp.where(some, total, 1.0)
        out_ref[b, :cols, :] = (summed * (1.0 / safe)).T.astype(jnp.bfloat16)
        level = jnp.where(some, top * SCALE + jnp.log2(safe), LOW)
        level = jnp.concatenate([level[:, j : j + HD] for j in range(0, cols, HD)], axis=0)
        high = level.astype(jnp.bfloat16).astype(jnp.float32)
        middle = (level - high).astype(jnp.bfloat16).astype(jnp.float32)
        unused = jnp.zeros((LEVELS - 3 * (cols // HD), HD), jnp.float32)
        pieces = jnp.concatenate([high, middle, level - high - middle, unused], axis=0)
        out_ref[b, cols:, :] = pieces.astype(jnp.bfloat16)

    blocks = q_ref.shape[0]

    @pl.when(info_ref[0] == 0)
    def _():
        @pl.loop(0, blocks)
        def _(b):
            finish(b, top_in[b, :, here], total_in[b, :, here], sum_in[b, :, here])

    @pl.when(info_ref[0] > 0)
    def _():
        at = 0
        for ref in (far_ref, prev_ref):
            rows = ref.shape[0] * ref.shape[1] * TOK
            flat = ref[...].reshape(rows, 2 * HD)
            k_s[at : at + rows, :] = flat[:, :HD]
            for j in range(0, rows, CHUNK):
                vt_s[:HD, at + j : at + j + CHUNK] = flat[j : j + CHUNK, HD:].T
            at += rows
        vt_s[HD:, :] = jnp.ones((ONES, at), jnp.bfloat16)

        def begin(b, slot):
            scores = score(k_s[...], stacked_heads(q_ref, b, part * heads, heads))
            score_s[slot] = scores
            top_s[slot] = jnp.max(scores, axis=0, keepdims=True)

        def end(b, slot):
            old = top_in[b, :, here]
            top = jnp.maximum(old, top_s[slot])
            both = weigh(vt_s[...], score_s[slot], top)
            factor = jnp.exp2((old - top) * SCALE)
            finish(
                b,
                top,
                total_in[b, :, here] * factor + both[HD : HD + 1],
                sum_in[b, :, here] * factor + both[:HD],
            )

        begin(0, 0)

        @pl.loop(0, blocks // 2)
        def _(i):
            begin(2 * i + 1, 1)
            end(2 * i, 0)
            begin(jnp.minimum(2 * i + 2, blocks - 1), 0)
            end(2 * i + 1, 1)


def join_kernel(*refs):
    parts_refs, out_ref = refs[:-1], refs[-1]
    cols = parts_refs[0].shape[1] - LEVELS
    rows, heads = cols // HD, cols // TOK
    for part, parts_ref in enumerate(parts_refs):
        for m in range(KVH):
            level = []
            for p in range(2):
                pieces = parts_ref[2 * m + p, cols:, :].astype(jnp.float32)
                level.append(
                    pieces[:rows] + pieces[rows : 2 * rows] + pieces[2 * rows : 3 * rows]
                )
            share = 1.0 / (1.0 + jnp.exp2(level[1] - level[0]))
            share = jnp.concatenate([share, jnp.zeros((8 - rows, HD), jnp.float32)], axis=0).T
            for h in range(heads):
                at = h * TOK
                first = parts_ref[2 * m, at : at + TOK, :].astype(jnp.float32)
                second = parts_ref[2 * m + 1, at : at + TOK, :].astype(jnp.float32)
                mine = share[at % HD : at % HD + TOK, at // HD : at // HD + 1]
                mixed = second + (first - second) * mine
                at = (m * GROUP + part * heads + h) * HD
                out_ref[:, at : at + HD] = mixed.astype(jnp.bfloat16)


def in_vmem():
    return pl.BlockSpec(memory_space=pltpu.VMEM)


def in_smem():
    return pl.BlockSpec(memory_space=pltpu.SMEM)


def tables(block_order):
    za, zb, zp = (lax.axis_index(name) for name in ("za", "zb", "zp"))
    stretch = lax.axis_index(STRETCHES)
    ids = lax.dynamic_index_in_dim(block_order, stretch, 2, keepdims=False)
    ids = ids.reshape(2, 2, lax.axis_size("za"), lax.axis_size("zb"), lax.axis_size("zp"))
    keys = lax.dynamic_index_in_dim(ids, zp, 4, keepdims=False)
    keys = jnp.where(zp == 1, keys[:, :, ::-1], keys)
    near = lax.dynamic_index_in_dim(keys, zb, 3, keepdims=False)
    other = lax.dynamic_index_in_dim(keys, 1 - zb, 3, keepdims=False)
    keys = jnp.stack([near, other]).transpose(0, 1, 3, 2).reshape(2, -1)
    queries = lax.dynamic_index_in_dim(ids, za, 2, keepdims=False)
    queries = lax.dynamic_index_in_dim(queries, zb, 2, keepdims=False).reshape(-1)
    place = jnp.sum(keys[:, None, :] < keys[:, :, None], axis=2, dtype=jnp.int32)
    slots = jnp.arange(keys.shape[1], dtype=jnp.int32)
    there = place[:, None, :] == slots[None, :, None]
    in_order = jnp.sum(jnp.where(there, keys[:, None, :], 0), axis=2)
    seen = jnp.sum(keys[:, None, :] <= queries[None, :, None], axis=2, dtype=jnp.int32)
    queries = jnp.broadcast_to(queries, seen.shape)
    stretches = jnp.broadcast_to(stretch, (2, 1))
    table = jnp.concatenate([place, in_order, queries, seen, stretches], axis=1)
    return table[0], table[1], stretch.reshape(1)


def along(block, axis, step, around):
    count = lax.axis_size(axis)
    route = [(i, (i + step) % count) for i in range(count) if around or i + step < count]
    return lax.ppermute(block, axis, route)


def body(queries, keys, values, block_order):
    tokens = queries.shape[0]
    lines = KVH
    params = pltpu.CompilerParams(vmem_limit_bytes=40 * MIB)
    pairs = lax.axis_size("zp")
    width = GROUP * HD
    kv = jnp.stack(
        [
            jnp.concatenate(
                [keys[:, m * HD : (m + 1) * HD], values[:, m * HD : (m + 1) * HD]], axis=1
            )
            for m in range(lines)
        ]
    )
    own = lax.all_to_all(kv, LINE, split_axis=0, concat_axis=0, tiled=True)
    info_near, info_other, stretch = tables(block_order)

    with jax.named_scope("pack_queries"):
        split = pl.pallas_call(
            pack_queries_kernel,
            out_shape=jax.ShapeDtypeStruct((lines * pairs, tokens, width), jnp.bfloat16),
            in_specs=[in_vmem()],
            out_specs=in_vmem(),
            compiler_params=params,
            cost_estimate=pl.CostEstimate(flops=0, bytes_accessed=2 * MIB, transcendentals=0),
        )(queries)
    own, split, info_near, info_other, stretch = lax.optimization_barrier(
        (own, split, info_near, info_other, stretch)
    )
    far = lax.all_gather(own, DEPTH, axis=0, axis_index_groups=FAR)
    lower, upper = far[:, :2], far[:, 2:]
    own_next = along(lower, RING, -1, True)
    own_prev = along(upper, RING, 1, True)
    query = lax.all_to_all(split, SHARE, split_axis=0, concat_axis=0, tiled=True)
    blocks = lines * pairs

    count = lax.axis_size(RING) * 2 * TOK
    state = [
        jax.ShapeDtypeStruct((blocks, 1, ROWS), jnp.float32),
        jax.ShapeDtypeStruct((blocks, 1, ROWS), jnp.float32),
        jax.ShapeDtypeStruct((blocks, HD, ROWS), jnp.float32),
    ]
    cost = pl.CostEstimate(
        flops=4 * blocks * ROWS * count * HD,
        bytes_accessed=4 * MIB,
        transcendentals=blocks * ROWS * count,
    )
    half = count // 2

    def own_part(info, lower, upper, *state_in):
        return pl.pallas_call(
            functools.partial(own_kernel, len(state_in) // 3),
            out_shape=state,
            in_specs=[in_smem()] + [in_vmem()] * (3 + len(state_in)),
            out_specs=[in_vmem()] * 3,
            scratch_shapes=[
                pltpu.VMEM((count, HD), jnp.bfloat16),
                pltpu.VMEM((count, HD), jnp.bfloat16),
                pltpu.VMEM((SIDE, count), jnp.bfloat16),
                pltpu.VMEM((TOK, ROWS), jnp.int32),
                pltpu.VMEM((4, half, ROWS), jnp.float32),
                pltpu.VMEM((4, 1, ROWS), jnp.float32),
                pltpu.VMEM((4, CHUNK, ROWS), jnp.float32),
                pltpu.VMEM((4, 1, ROWS), jnp.float32),
            ],
            compiler_params=params,
            cost_estimate=cost,
        )(info, query, lower, upper, *state_in)

    with jax.named_scope("own_near_first"):
        sums_1 = own_part(info_near, lower, upper)
    onward, *sums_1 = lax.optimization_barrier((upper, *sums_1))
    own_prev, sums_1[0] = lax.optimization_barrier((own_prev, sums_1[0]))
    earlier_prev = along(own_prev, STRETCHES, 1, False)
    earlier_far = along(onward, STRETCHES, 1, False)
    own_prev, lower, upper = lax.optimization_barrier((own_prev, lower, upper))
    with jax.named_scope("own_near_second"):
        sums_0 = own_part(info_near, lower, upper, *sums_1)
    with jax.named_scope("own_other"):
        sums = own_part(info_other, own_next, own_prev, *sums_0, *sums_1)
    cols = ROWS // PARTS
    joined = []
    for i in range(PARTS):
        with jax.named_scope("earlier_part"):
            part = pl.pallas_call(
                functools.partial(earlier_kernel, i),
                out_shape=jax.ShapeDtypeStruct((blocks, cols + LEVELS, HD), jnp.bfloat16),
                in_specs=[in_smem()] + [in_vmem()] * 6,
                out_specs=in_vmem(),
                scratch_shapes=[
                    pltpu.VMEM((count, HD), jnp.bfloat16),
                    pltpu.VMEM((SIDE, count), jnp.bfloat16),
                    pltpu.VMEM((2, count, cols), jnp.float32),
                    pltpu.VMEM((2, 1, cols), jnp.float32),
                ],
                compiler_params=params,
                cost_estimate=cost,
            )(stretch, query, earlier_prev, earlier_far, *sums)
        joined.append(lax.all_to_all(part, SHARE, split_axis=0, concat_axis=0, tiled=True))
    with jax.named_scope("join_parts"):
        return pl.pallas_call(
            join_kernel,
            out_shape=jax.ShapeDtypeStruct((tokens, lines * width), jnp.bfloat16),
            in_specs=[in_vmem()] * PARTS,
            out_specs=in_vmem(),
            compiler_params=params,
            cost_estimate=pl.CostEstimate(
                flops=3 * tokens * lines * width, bytes_accessed=2 * MIB, transcendentals=0
            ),
        )(*joined)


def solution(mesh):
    fine = Mesh(mesh.devices.reshape(2, 2, 4, 2, 2, 4, 2), AXES)
    rows = P(AXES, None)
    return jax.shard_map(
        body, mesh=fine, in_specs=(rows, rows, rows, P()), out_specs=rows, check_vma=False
    )
```
